32 devices in a mesh: expert: 8 (over z, x), tensor: 4 (over y, core).
Axes of the slice: x: 2, y: 2, z: 4, core: 2. Of those that a mesh axis runs over, the one named last changes fastest.
Arguments:
- tokens: bfloat16 [1024, 4096], P('expert'), may hold values from -6 to 6
- cotangent: bfloat16 [1024, 4096], P('expert'), may hold values from -6 to 6
- expert_ids: int32 [1024, 8], P('expert'), may hold values from 0 to 63, all different within a row; in each aligned block of 128 rows (0 to 127, 128 to 255, ...) at most 18 rows name the same one
- gate_probs: float32 [1024, 8], P('expert'), may hold values from 0.05 to 1
- w_gate: bfloat16 [64, 896, 4096], P('expert', 'tensor'), may hold values from -0.09375 to 0.09375
- w_up: bfloat16 [64, 896, 4096], P('expert', 'tensor'), may hold values from -0.09375 to 0.09375
- w_down: bfloat16 [64, 896, 4096], P('expert', 'tensor'), may hold values from -0.1875 to 0.1875
Outputs:
- mixed: bfloat16 [1024, 4096], P('expert')
- grad_tokens: bfloat16 [1024, 4096], P('expert')
The draws below stay inside these ranges and needn't reach their ends.
Inputs may be any that keep to these rules, and one draw needn't show every extreme that they name: `expert_ids`: each token names 8 different experts; the 128 tokens of one index of the expert axis name one expert at most 18 times, a bound that some block reaches.
All inputs are finite; a program needn't handle non-finite values.
Results may differ from the reference program's by a relative error of at most 0.017.
Values may be sent and summed in bfloat16 or wider, within the bound.
No kernel may reach another device: no remote copies, remote signals or barrier semaphores. Data moves between devices by JAX's collectives and lax.ppermute only.
A program may use at most 192 MiB of HBM per device.

```python
import math
import jax
import jax.numpy as jnp
import numpy as np
from jax import lax

D = 4096
HID = 896
TOP = 8
TOK_DEV = 128
EXPERTS = 64
TOKENS = 1024
CAP = 18
N_EXPERT = 8
N_TENSOR = 4


def level_of(stream_key, extent, cuts, smallest, largest):
    level, own = 1.0, jax.random.fold_in(stream_key, 6)
    for position, shards_of in cuts:
        heights = jnp.exp(jax.random.uniform(jax.random.fold_in(own, position), (shards_of,), jnp.float32, smallest / len(cuts), largest / len(cuts)))
        level = level * jnp.repeat(heights, extent[position] // shards_of).reshape([-1 if axis == position else 1 for axis in range(len(extent))])
    return level


def shared_out(key, own, number, rows, count, top, reach, slope):
    order = jax.random.permutation(key, count)
    crowded, usual = portions_of(count, rows * top, reach, slope, True), portions_of(count, rows * top, reach, slope, False)
    places = jnp.arange(count)

    def named(sizes, rotation):
        used = int((sizes > 0).sum())
        fixed = max(1, used // 4)
        shifted = fixed + (places - fixed + rotation * (used - fixed)) % max(1, count - fixed)
        return jnp.zeros((count,), jnp.int32).at[order[jnp.where(places < fixed, places, shifted)]].set(jnp.asarray(sizes, jnp.int32))

    sizes = jnp.where(number % 4 == 0, named(crowded, number // 4), named(usual, number - number // 4 - 1))
    mixed = jax.random.permutation(jax.random.fold_in(own, 3), count)
    donor, taker = mixed[0:count // 2 * 2:2], mixed[1:count // 2 * 2:2]
    slack = jnp.minimum(sizes[donor] - 1, reach - sizes[taker]) // 2
    slack = jnp.where((donor == order[0]) | (taker == order[0]) | (sizes[taker] == 0), 0, jnp.maximum(slack, 0))
    shifted = jax.random.randint(jax.random.fold_in(own, 4), (count // 2,), 0, 1 << 20) % (slack + 1)
    sizes = sizes.at[donor].add(-shifted).at[taker].add(shifted)
    items = jnp.searchsorted(jnp.cumsum(sizes), jnp.arange(rows * top), side="right").astype(jnp.int32)
    table = items.reshape(top, rows).T
    table = table[jax.random.permutation(jax.random.fold_in(own, 1), rows)]
    rotation = jax.random.randint(jax.random.fold_in(own, 2), (rows, 1), 0, top)
    return jnp.take_along_axis(table, (jnp.arange(top)[None, :] + rotation) % top, axis=1)


def portions_of(amount, total, most, slope, full):
    loads = [(1 << 20) // math.isqrt(rank ** slope) + 1 for rank in range(1, amount + 1)]
    largest = most if full else min(most, max(-(-total // amount), total * loads[0] // sum(loads)))
    least = 1 if total - largest >= amount - 1 else 0
    given, rest = [largest] + [least] * (amount - 1), total - largest - least * (amount - 1)
    while rest > 0:
        free = [i for i in range(1, amount) if given[i] < largest] or [i for i in range(1, amount) if given[i] < most]
        pool, remaining = sum([loads[i] for i in free]), rest
        for i in free:
            addition = min(most - given[i], max(1, remaining * loads[i] // pool), rest)
            given[i] = given[i] + addition
            rest = rest - addition
    return np.array(given)


def centred(key, extent, spread, reach, split=(), held_as=jnp.bfloat16):
    entries = spread * jax.random.normal(key, extent, jnp.float32)
    if split:
        entries = entries * level_of(key, extent, split, -0.22, 0.18)
    return jnp.clip(entries, -reach, reach).astype(held_as)


def setup_inputs(seed: int = 0) -> dict:
    key_list = jax.random.split(jax.random.key(seed), 8)
    tokens = centred(key_list[0], (TOKENS, D), 1.0, 6.0, ((0, 8),))
    cotangent = centred(key_list[1], (TOKENS, D), 1.0, 6.0, ((0, 8),))
    expert_ids_keys = jax.random.split(jax.random.fold_in(key_list[2], 1), TOKENS // TOK_DEV)
    expert_ids_turns = jax.random.permutation(jax.random.fold_in(key_list[2], 3), TOKENS // TOK_DEV)
    expert_ids = jax.vmap(lambda own, number: shared_out(jax.random.fold_in(key_list[2], 2), own, number, TOK_DEV, EXPERTS, TOP, CAP, 2))(expert_ids_keys, expert_ids_turns).reshape((TOKENS, TOP))
    gate_probs = jnp.clip(jnp.exp(math.log(1.0) - 2.9957323 * jax.random.uniform(key_list[3], (TOKENS, TOP), jnp.float32) ** level_of(key_list[3], (TOKENS, TOP), ((0, 8),), -0.2, 0.2)), 0.05, 1.0)
    w_gate = centred(key_list[4], (EXPERTS, HID, D), D ** -0.5, 0.09375, ((0, 8), (1, 4)))
    w_up = centred(key_list[5], (EXPERTS, HID, D), D ** -0.5, 0.09375, ((0, 8), (1, 4)))
    w_down = centred(key_list[6], (EXPERTS, HID, D), HID ** -0.5, 0.1875, ((0, 8), (1, 4)))
    return dict(tokens=tokens, cotangent=cotangent, expert_ids=expert_ids, gate_probs=gate_probs, w_gate=w_gate, w_up=w_up, w_down=w_down)


def block_product(operand, matrix, operand_two, matrix_two):
    row_count = operand.shape[0]
    block_size = matrix.shape[0] // N_TENSOR
    partial_value = jnp.einsum("rbh,bhd->rbd", operand.astype(jnp.float32).reshape(row_count, N_TENSOR, block_size), matrix.astype(jnp.float32).reshape(N_TENSOR, block_size, matrix.shape[1]))
    if operand_two is not None:
        partial_value = partial_value + jnp.einsum("rbh,bhd->rbd", operand_two.astype(jnp.float32).reshape(row_count, N_TENSOR, block_size), matrix_two.astype(jnp.float32).reshape(N_TENSOR, block_size, matrix_two.shape[1]))
    rounded = lax.optimization_barrier(partial_value.astype(jnp.bfloat16))
    return jnp.sum(rounded.astype(jnp.float32), axis=1).astype(jnp.bfloat16)


def reference(tokens, cotangent, expert_ids, gate_probs, w_gate, w_up, w_down):
    features = tokens.shape[1]
    pair_count = TOK_DEV * TOP
    flat_ids = expert_ids.reshape(N_EXPERT, pair_count)
    one_hot = (flat_ids[:, :, None] == jnp.arange(EXPERTS, dtype=jnp.int32)[None, None, :]).astype(jnp.int32)
    slot_index = jnp.sum(jnp.cumsum(one_hot, axis=1) * one_hot, axis=2) - 1
    source = jnp.arange(N_EXPERT, dtype=jnp.int32)[:, None] * jnp.ones((1, pair_count), jnp.int32)
    table_pos = (source * CAP + slot_index).astype(jnp.int32)
    token_index = (source * TOK_DEV + (jnp.arange(pair_count, dtype=jnp.int32) // TOP)[None, :]).astype(jnp.int32)
    row_table = jnp.full((EXPERTS, N_EXPERT * CAP), TOKENS, jnp.int32).at[flat_ids, table_pos].set(token_index)
    prob_table = jnp.zeros((EXPERTS, N_EXPERT * CAP), jnp.float32).at[flat_ids, table_pos].set(gate_probs.reshape(N_EXPERT, pair_count))
    tok_pad = jnp.concatenate([tokens, jnp.zeros((1, features), tokens.dtype)], 0)
    cot_pad = jnp.concatenate([cotangent, jnp.zeros((1, features), cotangent.dtype)], 0)

    def per_expert(packed):
        row_ids, prob_rows, gate_matrix, up_matrix, down_matrix = packed
        token_rows = tok_pad[row_ids]
        scaled_rows = (prob_rows[:, None] * cot_pad[row_ids].astype(jnp.float32)).astype(jnp.bfloat16)
        pre_gate = jnp.dot(token_rows, gate_matrix.T, preferred_element_type=jnp.float32)
        up_value = jnp.dot(token_rows, up_matrix.T, preferred_element_type=jnp.float32)
        sigmoid_gate = jax.nn.sigmoid(pre_gate)
        activated = pre_gate * sigmoid_gate
        hidden = (activated * up_value).astype(jnp.bfloat16)
        output_rows = block_product(hidden, down_matrix, None, None)
        grad_hidden = jnp.dot(scaled_rows, down_matrix.T, preferred_element_type=jnp.float32)
        grad_gate = (grad_hidden * up_value * sigmoid_gate * (1.0 + pre_gate * (1.0 - sigmoid_gate))).astype(jnp.bfloat16)
        grad_up = (grad_hidden * activated).astype(jnp.bfloat16)
        grad_rows = block_product(grad_gate, gate_matrix, grad_up, up_matrix)
        return output_rows, grad_rows

    outputs, gradients = lax.map(per_expert, (row_table, prob_table, w_gate, w_up, w_down))
    picked_out = outputs[flat_ids, table_pos].reshape(TOKENS, TOP, features)
    picked_grad = gradients[flat_ids, table_pos].reshape(TOKENS, TOP, features)
    mixed = jnp.einsum("nk,nkd->nd", gate_probs.astype(jnp.float32), picked_out.astype(jnp.float32)).astype(jnp.bfloat16)
    grad_tokens = jnp.sum(picked_grad.astype(jnp.float32), axis=1).astype(jnp.bfloat16)
    return mixed, grad_tokens
```

```python
import functools

import jax
import jax.numpy as jnp
from jax import lax
from jax.experimental import pallas as pl
from jax.experimental.pallas import tpu as pltpu
from jax.sharding import PartitionSpec as P

AXES = ("expert", "tensor")
CHUNK = 512
ROW_TILE = 16


def chip_moves():
    def pairs(step):
        found = []
        for z in range(4):
            for x in range(2):
                for y in range(2):
                    for core in range(2):
                        to_z, to_x, to_y, to_core = step(z, x, y, core)
                        source = (z * 2 + x) * 4 + y * 2 + core
                        found.append((source, ((to_z % 4) * 2 + to_x) * 4 + to_y * 2 + to_core))
        return found

    return dict(
        ahead=pairs(lambda z, x, y, core: (z + 1 - 2 * y, x, y, core)),
        back=pairs(lambda z, x, y, core: (z - 1 + 2 * y, x, y, core)),
        x=pairs(lambda z, x, y, core: (z, 1 - x, y, core)),
        y=pairs(lambda z, x, y, core: (z, x, 1 - y, core)),
        core=pairs(lambda z, x, y, core: (z, x, y, 1 - core)),
    )


MOVES = chip_moves()


def move(array, name):
    return lax.ppermute(array, AXES, MOVES[name])


def add(*terms):
    total = terms[0].astype(jnp.float32)
    for term in terms[1:]:
        total = total + term.astype(jnp.float32)
    return total.astype(jnp.bfloat16)


def spread(array, core, through_x):
    half = array.shape[1] // 2
    q0 = lax.dynamic_slice_in_dim(array, core * half, half, 1)
    own_other = lax.dynamic_slice_in_dim(array, (1 - core) * half, half, 1)
    q1, r0 = move(q0, "ahead"), move(q0, "x")
    q2, r1, q3 = move(q1, "ahead"), move(q1, "x"), move(q1, "y")
    r3 = move(r1, "y")
    r2 = move(q2, "x") if through_x else move(r1, "ahead")
    mine = [q0, r0, q1, r1, q2, r2, q3, r3]
    other = [own_other] + [move(block, "core") for block in mine[1:]]
    return mine + other


def collect(to_other, to_mine, core, through_x):
    arrived = move(to_other, "core")
    rows = to_mine.shape[0] // 8
    own, r0, q1, r1, q2, r2, q3, r3 = [
        add(to_mine[j * rows : (j + 1) * rows], arrived[j * rows : (j + 1) * rows]) for j in range(8)
    ]
    from_y_r, from_y_q, from_x = move(r3, "y"), move(q3, "y"), move(r0, "x")
    if through_x:
        r1 = add(r1, from_y_r)
        q2 = add(q2, move(r2, "x"))
    else:
        r1 = add(r1, from_y_r, move(r2, "back"))
    q1 = add(q1, from_y_q, move(r1, "x"), move(q2, "back"))
    own = add(own, from_x, move(q1, "back"))
    final = add(own, move(own, "y"))
    final_other = move(final, "core")
    return jnp.concatenate(
        [jnp.where(core == 0, final, final_other), jnp.where(core == 0, final_other, final)], axis=1
    )


def expert_kernel(backward, sources, group, experts, slots, half, *refs):
    core_ref, place_ref, place_t_ref, prob_ref = refs[:4]
    piece_refs = refs[4 : 4 + 2 * sources]
    gate_ref, up_ref, down_ref = refs[4 + 2 * sources : 7 + 2 * sources]
    first_ref, second_ref, other_ref, mine_ref, block_ref, rows_ref, sem_ref = refs[7 + 2 * sources :]
    step = pl.program_id(0)
    core = core_ref[0]
    tokens = block_ref.shape[1] // sources
    span = group * tokens
    groups = sources // group
    nt = (((1,), (1,)), ((), ()))

    @pl.when(step == 0)
    def _():
        def copy(side, j):
            place = block_ref.at[side, pl.ds(j * tokens, tokens)]
            return pltpu.make_async_copy(
                piece_refs[side * sources + j], place, sem_ref.at[side * sources + j]
            )

        for k in range(groups):
            for side in range(2):
                for j in range(k * group, (k + 1) * group):
                    copy(side, j).start()
        for k in range(groups):
            for side in range(2):
                for j in range(k * group, (k + 1) * group):
                    copy(side, j).wait()
                base = (core if side == 0 else 1 - core) * half

                @pl.loop(0, half // CHUNK)
                def _(i):
                    column = pl.multiple_of(i * CHUNK, CHUNK)
                    block = block_ref[side, pl.ds(k * span, span), pl.ds(column, CHUNK)]
                    picked = jnp.dot(place_ref[k], block, preferred_element_type=jnp.float32)
                    if backward:
                        picked = picked * prob_ref[k]
                    to = pl.multiple_of(base + column, CHUNK)
                    rows_ref[:, pl.ds(k * slots, slots), pl.ds(to, CHUNK)] = picked.astype(
                        jnp.bfloat16
                    ).reshape(experts, slots, CHUNK)

    @pl.when(step < experts)
    def _():
        rows = rows_ref[step]
        if backward:
            grad_hidden = lax.dot_general(rows, down_ref[0], nt, preferred_element_type=jnp.float32)
            left = (grad_hidden * first_ref[0]).astype(jnp.bfloat16)
            right = (grad_hidden * second_ref[0]).astype(jnp.bfloat16)
        else:
            pre_gate = lax.dot_general(rows, gate_ref[0], nt, preferred_element_type=jnp.float32)
            up_value = lax.dot_general(rows, up_ref[0], nt, preferred_element_type=jnp.float32)
            sigmoid = jax.nn.sigmoid(pre_gate)
            activated = pre_gate * sigmoid
            left = (activated * up_value).astype(jnp.bfloat16)
            first_ref[0] = up_value * sigmoid * (1.0 + pre_gate * (1.0 - sigmoid))
            second_ref[0] = activated

        @pl.loop(0, 2 * half // CHUNK)
        def _(i):
            columns = pl.ds(pl.multiple_of(i * CHUNK, CHUNK), CHUNK)
            if backward:
                result = jnp.dot(
                    left, gate_ref[0, :, columns], preferred_element_type=jnp.float32
                ) + jnp.dot(right, up_ref[0, :, columns], preferred_element_type=jnp.float32)
            else:
                result = jnp.dot(left, down_ref[0, :, columns], preferred_element_type=jnp.float32)
                result = result * prob_ref[0]
            rows_ref[step, :, columns] = result.astype(jnp.bfloat16)

    def combine(part, out_ref, side):
        base = (core if side == 0 else 1 - core) * half
        columns = pl.ds(pl.multiple_of(base + part * CHUNK, CHUNK), CHUNK)
        for k in range(groups):
            rows = rows_ref[:, pl.ds(k * slots, slots), columns].reshape(experts * slots, CHUNK)
            out_ref[pl.ds(k * span, span), :] = jnp.dot(
                place_t_ref[k], rows, preferred_element_type=jnp.float32
            ).astype(jnp.bfloat16)

    parts = half // CHUNK

    @pl.when((step >= experts) & (step < experts + parts))
    def _():
        combine(step - experts, other_ref, 1)

    @pl.when(step >= experts + parts)
    def _():
        combine(step - experts - parts, mine_ref, 0)


def expert_call(backward, core, place, place_t, prob, pieces, weights, factors, group):
    w_gate, w_up, w_down = weights
    experts, hidden, features = w_gate.shape
    sources = len(pieces) // 2
    tokens, half = pieces[0].shape
    groups, height, span = place.shape
    slots = height // experts
    total = groups * slots
    parts = half // CHUNK
    last = experts - 1
    whole = lambda shape: pl.BlockSpec(shape, lambda i, c: (0,) * len(shape))
    per_expert = lambda shape: pl.BlockSpec(shape, lambda i, c: (jnp.minimum(i, last), 0, 0))
    factor_spec = per_expert((1, total, hidden))
    factor_shape = jax.ShapeDtypeStruct((experts, total, hidden), jnp.float32)
    out_shape = jax.ShapeDtypeStruct((sources * tokens, half), jnp.bfloat16)
    out_specs = [
        pl.BlockSpec((sources * tokens, CHUNK), lambda i, c: (0, jnp.clip(i - experts, 0, parts - 1))),
        pl.BlockSpec(
            (sources * tokens, CHUNK), lambda i, c: (0, jnp.clip(i - experts - parts, 0, parts - 1))
        ),
    ]
    in_specs = [
        whole(place.shape),
        whole(place_t.shape),
        whole(prob.shape) if backward else per_expert((1, total, 1)),
    ]
    in_specs += [pl.BlockSpec(memory_space=pl.ANY)] * (2 * sources)
    in_specs += [per_expert((1, hidden, features))] * 3
    if backward:
        in_specs += [factor_spec, factor_spec]
        out_shapes = [out_shape, out_shape]
    else:
        out_specs = [factor_spec, factor_spec] + out_specs
        out_shapes = [factor_shape, factor_shape, out_shape, out_shape]
    flops = 2 * features * (3 * experts * total * hidden + 2 * groups * height * span)
    return pl.pallas_call(
        functools.partial(expert_kernel, backward, sources, group, experts, slots, half),
        grid_spec=pltpu.PrefetchScalarGridSpec(
            num_scalar_prefetch=1,
            grid=(experts + 2 * parts,),
            in_specs=in_specs,
            out_specs=out_specs,
            scratch_shapes=[
                pltpu.VMEM((2, sources * tokens, half), jnp.bfloat16),
                pltpu.VMEM((experts, total, features), jnp.bfloat16),
                pltpu.SemaphoreType.DMA((2 * sources,)),
            ],
        ),
        out_shape=out_shapes,
        compiler_params=pltpu.CompilerParams(vmem_limit_bytes=58 * 1024 * 1024),
        cost_estimate=pl.CostEstimate(
            flops=flops,
            bytes_accessed=3 * experts * hidden * features * 2 + 4 * sources * tokens * features,
            transcendentals=0,
        ),
        name="experts_backward" if backward else "experts_forward",
    )(core, place, place_t, prob, *pieces, w_gate, w_up, w_down, *factors)


def routing(expert_ids, gate_probs, local_experts, capacity, group):
    sources, tokens, _ = expert_ids.shape
    groups = sources // group
    slots = -(-group * capacity // ROW_TILE) * ROW_TILE
    first = lax.axis_index("expert") * local_experts
    matches = (expert_ids - first)[..., None] == jnp.arange(local_experts, dtype=jnp.int32)
    chosen = jnp.any(matches, axis=2)
    prob = jnp.sum(jnp.where(matches, gate_probs[..., None], 0.0), axis=2)
    earlier = jnp.arange(tokens)[:, None] > jnp.arange(tokens)[None, :]
    position = jnp.einsum(
        "tu,sue->ste",
        earlier.astype(jnp.bfloat16),
        chosen.astype(jnp.bfloat16),
        preferred_element_type=jnp.float32,
    ).astype(jnp.int32)
    position = position + (jnp.arange(sources, dtype=jnp.int32) % group * capacity)[:, None, None]
    position = jnp.where(chosen, position, -1)
    position = position.reshape(groups, group * tokens, local_experts)
    prob = prob.reshape(groups, group * tokens, local_experts).transpose(0, 2, 1)
    slot = jnp.arange(slots, dtype=jnp.int32)
    place = position.transpose(0, 2, 1)[:, :, None, :] == slot[:, None]
    place_t = position[:, :, :, None] == slot
    row_prob = jnp.sum(jnp.where(place, prob[:, :, None, :], 0.0), axis=3)
    height = local_experts * slots
    place = place.astype(jnp.bfloat16).reshape(groups, height, group * tokens)
    place_t = place_t.astype(jnp.bfloat16).reshape(groups, group * tokens, height)
    forward_prob = row_prob.transpose(1, 0, 2).reshape(local_experts, groups * slots, 1)
    return place, place_t, forward_prob, row_prob.reshape(groups, height, 1)


def body(fast, tokens, cotangent, expert_ids, gate_probs, w_gate, w_up, w_down):
    tok_count, features = tokens.shape
    top = expert_ids.shape[1]
    expert_devs = lax.axis_size("expert")
    local_experts = w_gate.shape[0]
    capacity = max(2, 9 * tok_count * top // (8 * local_experts * expert_devs))
    group = max(1, expert_devs // 4)
    weights = (w_gate, w_up, w_down)
    half = features // 2
    if fast:
        core = lax.axis_index("tensor") % 2
        choice = jnp.concatenate([expert_ids.astype(jnp.float32).T, gate_probs.T], axis=0)
        choice0 = jnp.stack([choice, move(choice, "x")])
        choice1 = move(choice0, "ahead")
        choice = jnp.concatenate([choice0, choice1, move(choice1, "ahead"), move(choice1, "y")])
        choice = choice.transpose(0, 2, 1)
        ids, probs = choice[..., :top].astype(jnp.int32), choice[..., top:]
        token_pieces = spread(tokens, core, True)
        cotangent_pieces = spread(cotangent, core, False)
    else:
        core = jnp.int32(0)

        def everywhere(array):
            return lax.all_gather(array, "expert", tiled=False)

        def split(array):
            blocks = everywhere(array)
            return [
                blocks[j, :, side * half : (side + 1) * half]
                for side in range(2)
                for j in range(expert_devs)
            ]

        ids, probs = everywhere(expert_ids), everywhere(gate_probs)
        token_pieces, cotangent_pieces = split(tokens), split(cotangent)
    place, place_t, forward_prob, backward_prob = routing(ids, probs, local_experts, capacity, group)
    core_ref = core.astype(jnp.int32).reshape(1)
    first, second, out_other, out_mine = expert_call(
        False, core_ref, place, place_t, forward_prob, token_pieces, weights, (), group
    )
    grad_other, grad_mine = expert_call(
        True, core_ref, place, place_t, backward_prob, cotangent_pieces, weights, (first, second), group
    )
    if fast:
        return collect(out_other, out_mine, core, True), collect(grad_other, grad_mine, core, False)

    def total(mine, other):
        partial = jnp.concatenate([mine, other], axis=1)
        own = lax.psum_scatter(partial, "expert", scatter_dimension=0, tiled=True)
        return lax.psum(own, "tensor")

    return total(out_mine, out_other), total(grad_mine, grad_other)


def solution(mesh):
    fast = mesh.shape["expert"] == 8 and mesh.shape["tensor"] == 4
    return jax.shard_map(
        functools.partial(body, fast),
        mesh=mesh,
        in_specs=(
            P("expert", None),
            P("expert", None),
            P("expert", None),
            P("expert", None),
            P("expert", "tensor", None),
            P("expert", "tensor", None),
            P("expert", "tensor", None),
        ),
        out_specs=(P("expert", None), P("expert", None)),
        check_vma=False,
    )
```

```python
import functools

import jax
import jax.numpy as jnp
import numpy as np
from jax import lax
from jax.experimental import pallas as pl
from jax.experimental.pallas import tpu as pltpu
from jax.sharding import PartitionSpec as P

AXES = ("expert", "tensor")
CHUNK = 512
ROW_TILE = 16
LANES = 128


def chip_moves():
    def pairs(step):
        found = []
        for z in range(4):
            for x in range(2):
                for y in range(2):
                    for core in range(2):
                        to_z, to_x, to_y, to_core = step(z, x, y, core)
                        source = (z * 2 + x) * 4 + y * 2 + core
                        found.append((source, ((to_z % 4) * 2 + to_x) * 4 + to_y * 2 + to_core))
        return found

    return dict(
        ahead=pairs(lambda z, x, y, core: (z + 1 - 2 * y, x, y, core)),
        back=pairs(lambda z, x, y, core: (z - 1 + 2 * y, x, y, core)),
        x=pairs(lambda z, x, y, core: (z, 1 - x, y, core)),
        y=pairs(lambda z, x, y, core: (z, x, 1 - y, core)),
        core=pairs(lambda z, x, y, core: (z, x, y, 1 - core)),
    )


MOVES = chip_moves()


def move(array, name):
    return lax.ppermute(array, AXES, MOVES[name])


def add(*terms):
    total = terms[0].astype(jnp.float32)
    for term in terms[1:]:
        total = total + term.astype(jnp.float32)
    return total.astype(jnp.bfloat16)


def halves(array, core):
    half = array.shape[1] // 2
    return [
        lax.dynamic_slice_in_dim(array, side * half, half, 1) for side in (core, 1 - core)
    ]


def enter_kernel(backward, parts, sources, group, slots, half, *refs):
    count = 1 if backward else 2
    core_ref = refs[0]
    place_refs = refs[1 : 1 + parts]
    piece_refs = refs[1 + parts : 1 + parts + 2 * sources]
    weight_refs = refs[1 + parts + 2 * sources : 1 + parts + 2 * sources + count]
    if backward:
        factor_refs, (left_ref, right_ref) = refs[1 + parts + 2 * sources + count : -7], refs[-7:-5]
    else:
        left_ref, first_ref, second_ref = refs[-8:-5]
    block_ref, rows_ref, buffer_ref, sem_ref, weight_sem_ref = refs[-5:]
    places = [ref.at[k] for ref in place_refs for k in range(ref.shape[0])]
    step = pl.program_id(0)
    core = core_ref[0]
    experts = rows_ref.shape[0]
    depth = buffer_ref.shape[1]
    tokens = block_ref.shape[1] // sources
    span = group * tokens
    nt = (((1,), (1,)), ((), ()))

    def piece_copy(side, j):
        return pltpu.make_async_copy(
            piece_refs[side * sources + j].at[:, pl.ds(0, half)],
            block_ref.at[side, pl.ds(j * tokens, tokens)],
            sem_ref.at[side * sources + j],
        )

    def weight_copy(n, expert):
        slot = lax.rem(expert, depth)
        return pltpu.make_async_copy(
            weight_refs[n].at[expert], buffer_ref.at[n, slot], weight_sem_ref.at[n, slot]
        )

    @pl.when(step == 0)
    def _():
        for k in range(sources // group):
            for side in range(2):
                for j in range(k * group, (k + 1) * group):
                    piece_copy(side, j).start()
            if k == 0:
                for n in range(count):
                    weight_copy(n, 0).start()
        for expert in range(1, depth):
            for n in range(count):
                weight_copy(n, expert).start()
        for k in range(sources // group):
            for side in range(2):
                for j in range(k * group, (k + 1) * group):
                    piece_copy(side, j).wait()
                base = (core if side == 0 else 1 - core) * half
                for column in range(0, half, CHUNK):
                    block = block_ref[side, pl.ds(k * span, span), pl.ds(column, CHUNK)]
                    picked = jnp.dot(places[k][...], block, preferred_element_type=jnp.float32)
                    to = pl.multiple_of(base + column, CHUNK)
                    rows_ref[:, pl.ds(k * slots, slots), pl.ds(to, CHUNK)] = picked.astype(
                        jnp.bfloat16
                    ).reshape(experts, slots, CHUNK)

    for n in range(count):
        weight_copy(n, step).wait()
    rows = rows_ref[step]
    slot = lax.rem(step, depth)
    products = [
        lax.dot_general(rows, buffer_ref[n, slot], nt, preferred_element_type=jnp.float32)
        for n in range(count)
    ]
    if backward:
        start = 0
        for first_ref, second_ref in zip(factor_refs[0::2], factor_refs[1::2]):
            span_rows = pl.ds(start, first_ref.shape[1])
            product = products[0][start : start + first_ref.shape[1]]
            left_ref[0, span_rows] = (product * first_ref[0]).astype(jnp.bfloat16)
            right_ref[0, span_rows] = (product * second_ref[0]).astype(jnp.bfloat16)
            start += first_ref.shape[1]
    else:
        pre_gate, up_value = products
        sigmoid = jax.nn.sigmoid(pre_gate)
        activated = pre_gate * sigmoid
        left_ref[0] = (activated * up_value).astype(jnp.bfloat16)
        first_ref[0] = up_value * sigmoid * (1.0 + pre_gate * (1.0 - sigmoid))
        second_ref[0] = activated

    @pl.when(step + depth < experts)
    def _():
        for n in range(count):
            weight_copy(n, step + depth).start()


def enter(backward, core, places, pieces, weights, factors):
    experts, hidden, features = weights[0].shape
    sources = len(pieces) // 2
    tokens, half = pieces[0].shape[0], features // 2
    _, height, span = places[0].shape
    groups = sum(place.shape[0] for place in places)
    slots = height // experts
    total = groups * slots
    depth = min(3, experts)
    per_expert = pl.BlockSpec((1, total, hidden), lambda i, c: (i, 0, 0))
    in_specs = [pl.BlockSpec(place.shape, lambda i, c: (0, 0, 0)) for place in places]
    in_specs += [pl.BlockSpec(memory_space=pl.ANY)] * (2 * sources + len(weights))
    in_specs += [
        pl.BlockSpec((1,) + factor.shape[1:], lambda i, c: (i, 0, 0)) for factor in factors
    ]
    values = jax.ShapeDtypeStruct((experts, total, hidden), jnp.bfloat16)
    exact = jax.ShapeDtypeStruct((experts, total, hidden), jnp.float32)
    out_shape = [values, values] if backward else [values, exact, exact]
    return pl.pallas_call(
        functools.partial(enter_kernel, backward, len(places), sources, span // tokens, slots, half),
        grid_spec=pltpu.PrefetchScalarGridSpec(
            num_scalar_prefetch=1,
            grid=(experts,),
            in_specs=in_specs,
            out_specs=[per_expert] * len(out_shape),
            scratch_shapes=[
                pltpu.VMEM((2, sources * tokens, half), jnp.bfloat16),
                pltpu.VMEM((experts, total, features), jnp.bfloat16),
                pltpu.VMEM((len(weights), depth, hidden, features), jnp.bfloat16),
                pltpu.SemaphoreType.DMA((2 * sources,)),
                pltpu.SemaphoreType.DMA((len(weights), depth)),
            ],
        ),
        out_shape=out_shape,
        compiler_params=pltpu.CompilerParams(vmem_limit_bytes=40 * 1024 * 1024),
        cost_estimate=pl.CostEstimate(
            flops=2 * features * (len(weights) * experts * total * hidden + groups * height * span),
            bytes_accessed=len(weights) * experts * hidden * features * 2
            + 2 * sources * tokens * features,
            transcendentals=0,
        ),
        name="enter_backward" if backward else "enter_forward",
    )(core, *places, *pieces, *weights, *factors)


def leave_kernel(parts, count, *refs):
    place_refs = refs[1 : 1 + parts]
    value_refs = refs[1 + parts : -2 - count]
    weight_refs = refs[-2 - count : -2]
    out_ref, rows_ref = refs[-2:]
    step = pl.program_id(0)
    experts, total, half = rows_ref.shape
    _, span, height = place_refs[0].shape
    places = [ref.at[k] for ref in place_refs for k in range(ref.shape[0])]
    slots = height // experts
    width = out_ref.shape[1]
    each = refs[-3].shape[0]
    turns = experts // each

    @pl.when(step < turns)
    def _():
        for n in range(each):
            expert = step * each + n
            values = [
                jnp.concatenate([ref[expert] for ref in value_refs[m::count]], axis=0)
                for m in range(count)
            ]
            for column in range(0, half, CHUNK):
                columns = pl.ds(column, CHUNK)
                result = sum(
                    jnp.dot(value, ref[n, :, columns], preferred_element_type=jnp.float32)
                    for value, ref in zip(values, weight_refs)
                )
                rows_ref[expert, :, columns] = result.astype(jnp.bfloat16)

    @pl.when(step >= turns)
    def _():
        base = (step - turns) * width
        for column in range(0, width, CHUNK // 2):
            columns = pl.ds(pl.multiple_of(base + column, CHUNK // 2), CHUNK // 2)
            for k in range(len(places)):
                rows = rows_ref[:, pl.ds(k * slots, slots), columns].reshape(height, CHUNK // 2)
                out_ref[pl.ds(k * span, span), pl.ds(column, CHUNK // 2)] = jnp.dot(
                    places[k][...], rows, preferred_element_type=jnp.float32
                ).astype(jnp.bfloat16)


def leave(side, places, values, weights):
    experts, hidden, features = weights[0].shape
    _, span, height = places[0].shape
    groups = sum(place.shape[0] for place in places)
    total = groups * (height // experts)
    half = features // 2
    width = half // 2
    each = 2 if experts % 2 == 0 else 1
    turns = experts // each
    whole = lambda shape: pl.BlockSpec(shape, lambda i, s: (0,) * len(shape))
    return pl.pallas_call(
        functools.partial(leave_kernel, len(places), len(weights)),
        grid_spec=pltpu.PrefetchScalarGridSpec(
            num_scalar_prefetch=1,
            grid=(turns + half // width,),
            in_specs=[whole(array.shape) for array in list(places) + list(values)]
            + [
                pl.BlockSpec(
                    (each, hidden, half), lambda i, s: (jnp.minimum(i, turns - 1), 0, s[0])
                )
            ]
            * len(weights),
            out_specs=pl.BlockSpec(
                (groups * span, width), lambda i, s: (0, jnp.maximum(i - turns, 0))
            ),
            scratch_shapes=[pltpu.VMEM((experts, total, half), jnp.bfloat16)],
        ),
        out_shape=jax.ShapeDtypeStruct((groups * span, half), jnp.bfloat16),
        compiler_params=pltpu.CompilerParams(vmem_limit_bytes=40 * 1024 * 1024),
        cost_estimate=pl.CostEstimate(
            flops=2 * half * (len(weights) * experts * total * hidden + groups * height * span),
            bytes_accessed=len(weights) * experts * hidden * half * 2 + 2 * groups * span * half,
            transcendentals=0,
        ),
        name="leave_forward" if len(weights) == 1 else "leave_backward",
    )(side, *places, *values, *weights)


def choice_columns(expert_ids, gate_probs):
    columns = jnp.concatenate([expert_ids.astype(jnp.float32), gate_probs], axis=1)
    columns = jnp.pad(columns, ((0, 0), (0, LANES - columns.shape[1])))
    return columns.astype(jnp.bfloat16)


def route_kernel(sources, group, capacity, *refs):
    first_ref = refs[0]
    choice_refs = refs[1 : 1 + sources]
    ids_ref, probs_ref, rows_ref, earlier_ref, expert_ref, slot_ref = refs[1 + sources : 7 + sources]
    place_ref, place_prob_ref, place_t_ref, place_t_prob_ref = refs[7 + sources :]
    tokens = earlier_ref.shape[0]
    dot = functools.partial(jnp.dot, preferred_element_type=jnp.float32)
    sought = expert_ref[...] + first_ref[0].astype(jnp.float32)
    for j in range(sources):
        k, s = divmod(j, group)
        choice = choice_refs[j][...]
        match = dot(choice, ids_ref[...]) == sought
        weight = jnp.where(match, dot(choice, probs_ref[...]), 0.0).astype(jnp.bfloat16)
        chosen = dot(jnp.where(match, 1.0, 0.0).astype(jnp.bfloat16), rows_ref[...])
        weight = dot(weight, rows_ref[...])
        position = dot(earlier_ref[...], chosen.astype(jnp.bfloat16)) + float(s * capacity)
        here = (chosen > 0.5) & (position == slot_ref[...])
        plain = jnp.where(here, 1.0, 0.0)
        weighted = jnp.where(here, weight, 0.0)
        span = pl.ds(s * tokens, tokens)
        place_t_ref[k, span, :] = plain.astype(jnp.bfloat16)
        place_t_prob_ref[k, span, :] = weighted.astype(jnp.bfloat16)
        place_ref[k, :, span] = plain.T.astype(jnp.bfloat16)
        place_prob_ref[k, :, span] = weighted.T.astype(jnp.bfloat16)


def route(first, choices, column, top, experts, capacity, group):
    sources, tokens = len(choices), choices[0].shape[0]
    groups = sources // group
    slots = -(-group * capacity // ROW_TILE) * ROW_TILE
    height, span = experts * slots, group * tokens
    lanes = np.arange(top * experts)
    rows = np.arange(height)
    columns = np.arange(LANES)[:, None]
    tables = [
        (columns == lanes // experts),
        (columns == lanes // experts + top),
        (lanes[:, None] % experts == rows // slots),
        (np.arange(tokens)[:, None] > np.arange(tokens)),
    ]
    tables = [jnp.asarray(table.astype(np.float32), jnp.bfloat16) for table in tables]
    tables += [
        jnp.asarray((lanes % experts).astype(np.float32)[None]),
        jnp.asarray((rows % slots).astype(np.float32)[None]),
    ]
    whole = lambda shape: pl.BlockSpec(shape, lambda i, f: (0,) * len(shape))
    by_row = jax.ShapeDtypeStruct((groups, height, span), jnp.bfloat16)
    by_token = jax.ShapeDtypeStruct((groups, span, height), jnp.bfloat16)
    out_shape = [by_row, by_row, by_token, by_token]
    return pl.pallas_call(
        functools.partial(route_kernel, sources, group, capacity),
        grid_spec=pltpu.PrefetchScalarGridSpec(
            num_scalar_prefetch=1,
            grid=(1,),
            in_specs=[pl.BlockSpec((tokens, LANES), lambda i, f: (0, column))] * sources
            + [whole(table.shape) for table in tables],
            out_specs=[whole(shape.shape) for shape in out_shape],
        ),
        out_shape=out_shape,
        compiler_params=pltpu.CompilerParams(vmem_limit_bytes=32 * 1024 * 1024),
        name="route",
    )(first, *choices, *tables)


def body(fast, tokens, cotangent, expert_ids, gate_probs, w_gate, w_up, w_down):
    tok_count, features = tokens.shape
    top = expert_ids.shape[1]
    expert_devs = lax.axis_size("expert")
    local_experts = w_gate.shape[0]
    capacity = max(2, 9 * tok_count * top // (8 * local_experts * expert_devs))
    group = max(1, expert_devs // 4)
    half = features // 2
    first = (lax.axis_index("expert") * local_experts).astype(jnp.int32).reshape(1)
    routed = functools.partial(
        route, first, top=top, experts=local_experts, capacity=capacity, group=group
    )
    own_choices = choice_columns(expert_ids, gate_probs)
    if fast:
        return exchange(
            routed, own_choices, tokens, cotangent, w_gate, w_up, w_down
        )

    def split(array):
        blocks = lax.all_gather(array, "expert")
        return [
            blocks[j, :, side * half : (side + 1) * half]
            for side in range(2)
            for j in range(expert_devs)
        ]

    choices = lax.all_gather(own_choices, "expert")
    place, place_prob, place_t, place_t_prob = routed([choices[j] for j in range(expert_devs)], 0)
    zero = jnp.zeros((1,), jnp.int32)
    hidden, *factors = enter(False, zero, [place], split(tokens), (w_gate, w_up), ())
    values = enter(True, zero, [place_prob], split(cotangent), (w_down,), factors)

    def total(table, values, weights):
        partial = jnp.concatenate(
            [leave(zero + side, [table], values, weights) for side in range(2)], axis=1
        )
        own = lax.psum_scatter(partial, "expert", scatter_dimension=0, tiled=True)
        return lax.psum(own, "tensor")

    return total(place_t_prob, (hidden,), (w_down,)), total(place_t, values, (w_gate, w_up))


def exchange(routed, own_choices, tokens, cotangent, w_gate, w_up, w_down):
    half = tokens.shape[1] // 2
    core = lax.axis_index("tensor") % 2
    mine = core.astype(jnp.int32).reshape(1)
    order = ("q0", "r0", "q1", "r1", "q2", "r2", "q3", "r3")

    def phase(live, moves, far=(), **made):
        moved = {name: move(live[old], how) for name, (old, how) in moves.items()}
        moved.update({name + "_far": move(live[name], "core") for name in far})
        return lax.optimization_barrier({**live, **moved, **made})

    def pieces(live, kind, names):
        return [live[kind + name] for name in names] + [live[kind + name + "_far"] for name in names]

    def enter_tokens(live, names):
        tables = live["near" if names is near else "late"]
        return enter(False, live["mine"], tables[:1], pieces(live, "t", names), (w_gate, w_up), ())

    near, late = order[:4], order[4:]
    tq0, tq0_far = halves(tokens, core)
    live = dict(mine=mine, tq0=jnp.concatenate([tq0, own_choices], axis=1), tq0_far=tq0_far)
    cq0, cq0_far = halves(cotangent, core)
    live = phase(live, dict(tq1=("tq0", "ahead"), tr0=("tq0", "x")), cq0=cq0, cq0_far=cq0_far)
    live = phase(
        live,
        dict(tq2=("tq1", "ahead"), tr1=("tq1", "x"), tq3=("tq1", "y")),
        far=("tr0", "tq1"),
    )
    tables = routed([live["t" + name] for name in near], half // LANES)
    live = phase(live, {}, far=("tr1",), near=tables)
    live = phase(
        live,
        dict(tr2=("tq2", "x"), tr3=("tr1", "y"), cq1=("cq0", "ahead")),
        far=("tq2", "tq3"),
        near_values=enter_tokens(live, near),
    )
    tables = routed([live["t" + name] for name in late], half // LANES)
    live = phase(live, {}, far=("tr2", "tr3"), late=tables)
    live = phase(
        live,
        dict(cq2=("cq1", "ahead"), cr1=("cq1", "x"), cq3=("cq1", "y")),
        far=("cq1",),
        late_values=enter_tokens(live, late),
    )
    live = {name: value for name, value in live.items() if name[0] != "t"}

    def leave_tokens(live, side):
        tables = [live["near"][3], live["late"][3]]
        return leave(side, tables, [live["near_values"][0], live["late_values"][0]], (w_down,))

    live = phase(
        live,
        dict(cr0=("cq0", "x"), cr2=("cr1", "ahead"), cr3=("cr1", "y")),
        far=("cq2", "cr1"),
        o_far=leave_tokens(live, 1 - live["mine"]),
    )
    live = phase(
        live,
        dict(o_new=("o_far", "core")),
        far=("cq3", "cr0", "cr2", "cr3"),
        o_near=leave_tokens(live, live["mine"]),
    )
    live.update(merge("o", live.pop("o_new"), live.pop("o_near")))
    del live["o_far"]
    live = lax.optimization_barrier(live)
    place_t = [live["near"][2], live["late"][2]]
    values = enter(
        True,
        live["mine"],
        [live["near"][1], live["late"][1]],
        pieces(live, "c", order),
        (w_down,),
        list(live["near_values"][1:]) + list(live["late_values"][1:]),
    )
    live = {name: value for name, value in live.items() if name[0] in "mo"}
    live = phase(
        live, dict(y=("or3", "y"), z=("or2", "back"), x=("or0", "x")), values=tuple(values)
    )
    live["or1"] = add(live["or1"], live["y"], live["z"])
    g_far = leave(1 - live["mine"], place_t, live["values"], (w_gate, w_up))
    live = phase(
        live, dict(y1=("oq3", "y"), x1=("or1", "x"), z1=("oq2", "back")), g_far=g_far
    )
    live["oq1"] = add(live["oq1"], live["y1"], live["x1"], live["z1"])
    g_near = leave(live["mine"], place_t, live["values"], (w_gate, w_up))
    live = phase(live, dict(g_new=("g_far", "core"), z2=("oq1", "back")), g_near=g_near)
    own = add(live["oq0"], live["x"], live["z2"])
    live = dict(own=own, **merge("g", live["g_new"], live["g_near"]))
    live = phase(live, dict(y=("gr3", "y"), z=("gr2", "back"), x=("gr0", "x")))
    live["gr1"] = add(live["gr1"], live["y"], live["z"])
    live = phase(live, dict(y1=("gq3", "y"), x1=("gr1", "x"), z1=("gq2", "back")))
    live["gq1"] = add(live["gq1"], live["y1"], live["x1"], live["z1"])
    live = phase(live, dict(z2=("gq1", "back"), far=("own", "y")))
    mixed = add(live["own"], live["far"])
    own = add(live["gq0"], live["x"], live["z2"])
    grad_tokens = add(own, move(own, "y"))
    return whole_rows(mixed, core), whole_rows(grad_tokens, core)


def merge(kind, arrived, own):
    rows = own.shape[0] // 8
    names = ("q0", "r0", "q1", "r1", "q2", "r2", "q3", "r3")
    return {
        kind + name: add(own[j * rows : (j + 1) * rows], arrived[j * rows : (j + 1) * rows])
        for j, name in enumerate(names)
    }


def whole_rows(own, core):
    far = move(own, "core")
    return jnp.concatenate([jnp.where(core == 0, own, far), jnp.where(core == 0, far, own)], axis=1)


def solution(mesh):
    fast = mesh.shape["expert"] == 8 and mesh.shape["tensor"] == 4
    return jax.shard_map(
        functools.partial(body, fast),
        mesh=mesh,
        in_specs=(
            P("expert", None),
            P("expert", None),
            P("expert", None),
            P("expert", None),
            P("expert", "tensor", None),
            P("expert", "tensor", None),
            P("expert", "tensor", None),
        ),
        out_specs=(P("expert", None), P("expert", None)),
        check_vma=False,
    )
```

```python
import functools

import jax
import jax.numpy as jnp
import numpy as np
from jax import lax
from jax.experimental import pallas as pl
from jax.experimental.pallas import tpu as pltpu
from jax.sharding import PartitionSpec as P

AXES = ("expert", "tensor")
CHUNK = 512
ROW_TILE = 16
LANES = 128


def chip_moves():
    def pairs(step):
        found = []
        for z in range(4):
            for x in range(2):
                for y in range(2):
                    for core in range(2):
                        to_z, to_x, to_y, to_core = step(z, x, y, core)
                        source = (z * 2 + x) * 4 + y * 2 + core
                        found.append((source, ((to_z % 4) * 2 + to_x) * 4 + to_y * 2 + to_core))
        return found

    return dict(
        ahead=pairs(lambda z, x, y, core: (z + 1 - 2 * y, x, y, core)),
        back=pairs(lambda z, x, y, core: (z - 1 + 2 * y, x, y, core)),
        x=pairs(lambda z, x, y, core: (z, 1 - x, y, core)),
        y=pairs(lambda z, x, y, core: (z, x, 1 - y, core)),
        core=pairs(lambda z, x, y, core: (z, x, y, 1 - core)),
    )


MOVES = chip_moves()


def move(array, name):
    return lax.ppermute(array, AXES, MOVES[name])


def add(*terms):
    total = terms[0].astype(jnp.float32)
    for term in terms[1:]:
        total = total + term.astype(jnp.float32)
    return total.astype(jnp.bfloat16)


def halves(array, core):
    half = array.shape[1] // 2
    return [
        lax.dynamic_slice_in_dim(array, side * half, half, 1) for side in (core, 1 - core)
    ]


def table_copies(refs, table_ref, sem_ref):
    copies, start = [], 0
    for n, ref in enumerate(refs):
        place = table_ref.at[pl.ds(start, ref.shape[0])]
        copies.append(pltpu.make_async_copy(ref, place, sem_ref.at[n]))
        start += ref.shape[0]
    return copies


def enter_kernel(backward, parts, sources, group, slots, half, *refs):
    count = 1 if backward else 2
    core_ref = refs[0]
    place_refs = refs[1 : 1 + parts]
    piece_refs = refs[1 + parts : 1 + parts + 2 * sources]
    weight_refs = refs[1 + parts + 2 * sources : 1 + parts + 2 * sources + count]
    if backward:
        factor_refs, (left_ref, right_ref) = refs[1 + parts + 2 * sources + count : -9], refs[-9:-7]
    else:
        left_ref, first_ref, second_ref = refs[-10:-7]
    block_ref, rows_ref, buffer_ref, table_ref, sem_ref, weight_sem_ref, table_sem_ref = refs[-7:]
    step = pl.program_id(0)
    core = core_ref[0]
    experts = rows_ref.shape[0]
    depth = buffer_ref.shape[1]
    tokens = block_ref.shape[1] // sources
    span = group * tokens
    nt = (((1,), (1,)), ((), ()))

    def piece_copy(side, j):
        return pltpu.make_async_copy(
            piece_refs[side * sources + j].at[:, pl.ds(0, half)],
            block_ref.at[side, pl.ds(j * tokens, tokens)],
            sem_ref.at[side * sources + j],
        )

    def weight_copy(n, expert):
        slot = lax.rem(expert, depth)
        return pltpu.make_async_copy(
            weight_refs[n].at[expert], buffer_ref.at[n, slot], weight_sem_ref.at[n, slot]
        )

    @pl.when(step == 0)
    def _():
        tables = table_copies(place_refs, table_ref, table_sem_ref)
        for copy in tables:
            copy.start()
        for k in range(sources // group):
            for side in range(2):
                for j in range(k * group, (k + 1) * group):
                    piece_copy(side, j).start()
        for copy in tables:
            copy.wait()
        for k in range(sources // group):
            for side in range(2):
                for j in range(k * group, (k + 1) * group):
                    piece_copy(side, j).wait()
                if 2 * k + side < depth:
                    for n in range(count):
                        weight_copy(n, 2 * k + side).start()
                base = (core if side == 0 else 1 - core) * half
                for column in range(0, half, CHUNK):
                    block = block_ref[side, pl.ds(k * span, span), pl.ds(column, CHUNK)]
                    picked = jnp.dot(table_ref[k], block, preferred_element_type=jnp.float32)
                    to = pl.multiple_of(base + column, CHUNK)
                    rows_ref[:, pl.ds(k * slots, slots), pl.ds(to, CHUNK)] = picked.astype(
                        jnp.bfloat16
                    ).reshape(experts, slots, CHUNK)

    for n in range(count):
        weight_copy(n, step).wait()
    rows = rows_ref[step]
    slot = lax.rem(step, depth)
    products = [
        lax.dot_general(rows, buffer_ref[n, slot], nt, preferred_element_type=jnp.float32)
        for n in range(count)
    ]
    if backward:
        start = 0
        for first_ref, second_ref in zip(factor_refs[0::2], factor_refs[1::2]):
            span_rows = pl.ds(start, first_ref.shape[1])
            product = products[0][start : start + first_ref.shape[1]]
            left_ref[0, span_rows] = (product * first_ref[0]).astype(jnp.bfloat16)
            right_ref[0, span_rows] = (product * second_ref[0]).astype(jnp.bfloat16)
            start += first_ref.shape[1]
    else:
        pre_gate, up_value = products
        sigmoid = jax.nn.sigmoid(pre_gate)
        activated = pre_gate * sigmoid
        left_ref[0] = (activated * up_value).astype(jnp.bfloat16)
        first_ref[0] = up_value * sigmoid * (1.0 + pre_gate * (1.0 - sigmoid))
        second_ref[0] = activated

    @pl.when(step + depth < experts)
    def _():
        for n in range(count):
            weight_copy(n, step + depth).start()


def enter(backward, core, places, pieces, weights, factors):
    experts, hidden, features = weights[0].shape
    sources = len(pieces) // 2
    tokens, half = pieces[0].shape[0], features // 2
    _, height, span = places[0].shape
    groups = sum(place.shape[0] for place in places)
    slots = height // experts
    total = groups * slots
    depth = min(3, experts, 2 * groups)
    per_expert = pl.BlockSpec((1, total, hidden), lambda i, c: (i, 0, 0))
    in_specs = [pl.BlockSpec(memory_space=pl.ANY)] * (len(places) + 2 * sources + len(weights))
    in_specs += [
        pl.BlockSpec((1,) + factor.shape[1:], lambda i, c: (i, 0, 0)) for factor in factors
    ]
    values = jax.ShapeDtypeStruct((experts, total, hidden), jnp.bfloat16)
    exact = jax.ShapeDtypeStruct((experts, total, hidden), jnp.float32)
    out_shape = [values, values] if backward else [values, exact, exact]
    return pl.pallas_call(
        functools.partial(enter_kernel, backward, len(places), sources, span // tokens, slots, half),
        grid_spec=pltpu.PrefetchScalarGridSpec(
            num_scalar_prefetch=1,
            grid=(experts,),
            in_specs=in_specs,
            out_specs=[per_expert] * len(out_shape),
            scratch_shapes=[
                pltpu.VMEM((2, sources * tokens, half), jnp.bfloat16),
                pltpu.VMEM((experts, total, features), jnp.bfloat16),
                pltpu.VMEM((len(weights), depth, hidden, features), jnp.bfloat16),
                pltpu.VMEM((groups, height, span), jnp.bfloat16),
                pltpu.SemaphoreType.DMA((2 * sources,)),
                pltpu.SemaphoreType.DMA((len(weights), depth)),
                pltpu.SemaphoreType.DMA((len(places),)),
            ],
        ),
        out_shape=out_shape,
        compiler_params=pltpu.CompilerParams(vmem_limit_bytes=(38 if backward else 46) * 1024 * 1024),
        cost_estimate=pl.CostEstimate(
            flops=128 * features * (len(weights) * experts * total * hidden + groups * height * span),
            bytes_accessed=len(weights) * experts * hidden * features * 2
            + 2 * sources * tokens * features,
            transcendentals=0,
        ),
        name="enter_backward" if backward else "enter_forward",
    )(core, *places, *pieces, *weights, *factors)


def leave_kernel(parts, count, *refs):
    place_refs = refs[1 : 1 + parts]
    value_refs = refs[1 + parts : -2 - count]
    weight_refs = refs[-2 - count : -2]
    out_ref, rows_ref = refs[-2:]
    step = pl.program_id(0)
    experts, total, half = rows_ref.shape
    _, span, height = place_refs[0].shape
    places = [ref.at[k] for ref in place_refs for k in range(ref.shape[0])]
    slots = height // experts
    width = out_ref.shape[1]
    each = refs[-3].shape[0]
    turns = experts // each

    @pl.when(step < turns)
    def _():
        for n in range(each):
            expert = step * each + n
            values = [
                jnp.concatenate([ref[expert] for ref in value_refs[m::count]], axis=0)
                for m in range(count)
            ]
            for column in range(0, half, CHUNK):
                columns = pl.ds(column, CHUNK)
                result = sum(
                    jnp.dot(value, ref[n, :, columns], preferred_element_type=jnp.float32)
                    for value, ref in zip(values, weight_refs)
                )
                rows_ref[expert, :, columns] = result.astype(jnp.bfloat16)

    @pl.when(step >= turns)
    def _():
        base = (step - turns) * width
        for column in range(0, width, CHUNK // 2):
            columns = pl.ds(pl.multiple_of(base + column, CHUNK // 2), CHUNK // 2)
            for k in range(len(places)):
                rows = rows_ref[:, pl.ds(k * slots, slots), columns].reshape(height, CHUNK // 2)
                out_ref[pl.ds(k * span, span), pl.ds(column, CHUNK // 2)] = jnp.dot(
                    places[k][...], rows, preferred_element_type=jnp.float32
                ).astype(jnp.bfloat16)


def leave(side, places, values, weights):
    experts, hidden, features = weights[0].shape
    _, span, height = places[0].shape
    groups = sum(place.shape[0] for place in places)
    total = groups * (height // experts)
    half = features // 2
    width = half // 2
    each = 2 if experts % 2 == 0 else 1
    turns = experts // each
    whole = lambda shape: pl.BlockSpec(shape, lambda i, s: (0,) * len(shape))
    return pl.pallas_call(
        functools.partial(leave_kernel, len(places), len(weights)),
        grid_spec=pltpu.PrefetchScalarGridSpec(
            num_scalar_prefetch=1,
            grid=(turns + half // width,),
            in_specs=[whole(array.shape) for array in list(places) + list(values)]
            + [
                pl.BlockSpec(
                    (each, hidden, half),
                    functools.partial(
                        lambda wide, i, s: (jnp.minimum(i, turns - 1), 0, s[0] * wide),
                        int(weight.shape[2] > half),
                    ),
                )
                for weight in weights
            ],
            out_specs=pl.BlockSpec(
                (groups * span, width), lambda i, s: (0, jnp.maximum(i - turns, 0))
            ),
            scratch_shapes=[pltpu.VMEM((experts, total, half), jnp.bfloat16)],
        ),
        out_shape=jax.ShapeDtypeStruct((groups * span, half), jnp.bfloat16),
        compiler_params=pltpu.CompilerParams(vmem_limit_bytes=(46 if len(weights) < 4 else 40) * 1024 * 1024),
        cost_estimate=pl.CostEstimate(
            flops=128 * half * (len(weights) * experts * total * hidden + groups * height * span),
            bytes_accessed=len(weights) * experts * hidden * half * 2 + 2 * groups * span * half,
            transcendentals=0,
        ),
        name="leave",
    )(side, *places, *values, *weights)


def choice_columns(expert_ids, gate_probs):
    columns = jnp.concatenate([expert_ids.astype(jnp.float32), gate_probs], axis=1)
    columns = jnp.pad(columns, ((0, 0), (0, LANES - columns.shape[1])))
    return columns.astype(jnp.bfloat16)


def route_kernel(sources, group, capacity, *refs):
    first_ref = refs[0]
    choice_refs = refs[1 : 1 + sources]
    ids_ref, probs_ref, rows_ref, earlier_ref, expert_ref, slot_ref = refs[1 + sources : 7 + sources]
    place_ref, place_prob_ref, place_t_ref, place_t_prob_ref = refs[7 + sources :]
    tokens = earlier_ref.shape[0]
    dot = functools.partial(jnp.dot, preferred_element_type=jnp.float32)
    sought = expert_ref[...] + first_ref[0].astype(jnp.float32)
    for j in range(sources):
        k, s = divmod(j, group)
        choice = choice_refs[j][...]
        match = dot(choice, ids_ref[...]) == sought
        weight = jnp.where(match, dot(choice, probs_ref[...]), 0.0).astype(jnp.bfloat16)
        chosen = dot(jnp.where(match, 1.0, 0.0).astype(jnp.bfloat16), rows_ref[...])
        weight = dot(weight, rows_ref[...])
        position = dot(earlier_ref[...], chosen.astype(jnp.bfloat16)) + float(s * capacity)
        here = (chosen > 0.5) & (position == slot_ref[...])
        plain = jnp.where(here, 1.0, 0.0)
        weighted = jnp.where(here, weight, 0.0)
        span = pl.ds(s * tokens, tokens)
        place_t_ref[k, span, :] = plain.astype(jnp.bfloat16)
        place_t_prob_ref[k, span, :] = weighted.astype(jnp.bfloat16)
        place_ref[k, :, span] = plain.T.astype(jnp.bfloat16)
        place_prob_ref[k, :, span] = weighted.T.astype(jnp.bfloat16)


def route(first, choices, column, top, experts, capacity, group):
    sources, tokens = len(choices), choices[0].shape[0]
    groups = sources // group
    slots = -(-group * capacity // ROW_TILE) * ROW_TILE
    height, span = experts * slots, group * tokens
    lanes = np.arange(top * experts)
    rows = np.arange(height)
    columns = np.arange(LANES)[:, None]
    tables = [
        (columns == lanes // experts),
        (columns == lanes // experts + top),
        (lanes[:, None] % experts == rows // slots),
        (np.arange(tokens)[:, None] > np.arange(tokens)),
    ]
    tables = [jnp.asarray(table.astype(np.float32), jnp.bfloat16) for table in tables]
    tables += [
        jnp.asarray((lanes % experts).astype(np.float32)[None]),
        jnp.asarray((rows % slots).astype(np.float32)[None]),
    ]
    whole = lambda shape: pl.BlockSpec(shape, lambda i, f: (0,) * len(shape))
    by_row = jax.ShapeDtypeStruct((groups, height, span), jnp.bfloat16)
    by_token = jax.ShapeDtypeStruct((groups, span, height), jnp.bfloat16)
    out_shape = [by_row, by_row, by_token, by_token]
    return pl.pallas_call(
        functools.partial(route_kernel, sources, group, capacity),
        grid_spec=pltpu.PrefetchScalarGridSpec(
            num_scalar_prefetch=1,
            grid=(1,),
            in_specs=[pl.BlockSpec((tokens, LANES), lambda i, f: (0, column))] * sources
            + [whole(table.shape) for table in tables],
            out_specs=[whole(shape.shape) for shape in out_shape],
        ),
        out_shape=out_shape,
        compiler_params=pltpu.CompilerParams(vmem_limit_bytes=32 * 1024 * 1024),
        name="route",
    )(first, *choices, *tables)


def body(fast, tokens, cotangent, expert_ids, gate_probs, w_gate, w_up, w_down):
    tok_count, features = tokens.shape
    top = expert_ids.shape[1]
    expert_devs = lax.axis_size("expert")
    local_experts = w_gate.shape[0]
    capacity = max(2, 9 * tok_count * top // (8 * local_experts * expert_devs))
    group = max(1, expert_devs // 4)
    half = features // 2
    first = (lax.axis_index("expert") * local_experts).astype(jnp.int32).reshape(1)
    routed = functools.partial(
        route, first, top=top, experts=local_experts, capacity=capacity, group=group
    )
    own_choices = choice_columns(expert_ids, gate_probs)
    if fast:
        return exchange(
            routed, own_choices, tokens, cotangent, w_gate, w_up, w_down
        )

    def split(array):
        blocks = lax.all_gather(array, "expert")
        return [
            blocks[j, :, side * half : (side + 1) * half]
            for side in range(2)
            for j in range(expert_devs)
        ]

    choices = lax.all_gather(own_choices, "expert")
    place, place_prob, place_t, place_t_prob = routed([choices[j] for j in range(expert_devs)], 0)
    zero = jnp.zeros((1,), jnp.int32)
    hidden, *factors = enter(False, zero, [place], split(tokens), (w_gate, w_up), ())
    values = enter(True, zero, [place_prob], split(cotangent), (w_down,), factors)

    def total(table, values, weights):
        partial = jnp.concatenate(
            [leave(zero + side, [table], values, weights) for side in range(2)], axis=1
        )
        own = lax.psum_scatter(partial, "expert", scatter_dimension=0, tiled=True)
        return lax.psum(own, "tensor")

    return total(place_t_prob, (hidden,), (w_down,)), total(place_t, values, (w_gate, w_up))


def exchange(routed, own_choices, tokens, cotangent, w_gate, w_up, w_down):
    half = tokens.shape[1] // 2
    core = lax.axis_index("tensor") % 2
    mine = core.astype(jnp.int32).reshape(1)
    order = ("q0", "r0", "q1", "r1", "q2", "r2", "q3", "r3")

    def phase(live, moves, far=(), **made):
        moved = {name: move(live[old], how) for name, (old, how) in moves.items()}
        moved.update({name + "_far": move(live[name], "core") for name in far})
        return lax.optimization_barrier({**live, **moved, **made})

    def pieces(live, kind, names):
        return [live[kind + name] for name in names] + [live[kind + name + "_far"] for name in names]

    def enter_tokens(live, names):
        tables = live["near" if names is near else "late"]
        return enter(False, live["mine"], tables[:1], pieces(live, "t", names), (w_gate, w_up), ())

    def sibling_half(weight):
        return lax.dynamic_slice_in_dim(weight, (1 - core) * half, half, 2)

    def block(live, kind, name):
        rows = tokens.shape[0]
        start = order.index(name) * rows
        return live[kind][start : start + rows]

    near, late = order[:4], order[4:]
    tq0, tq0_far = halves(tokens, core)
    live = dict(mine=mine, tq0=jnp.concatenate([tq0, own_choices], axis=1), tq0_far=tq0_far)
    cq0, cq0_far = halves(cotangent, core)
    live = phase(
        live,
        dict(tq1=("tq0", "ahead"), tr0=("tq0", "x")),
        cq0=cq0,
        cq0_far=cq0_far,
        down=sibling_half(w_down),
        gate=sibling_half(w_gate),
    )
    live = phase(
        live,
        dict(tq2=("tq1", "ahead"), tr1=("tq1", "x"), tq3=("tq1", "y")),
        far=("tr0", "tq1"),
        up=sibling_half(w_up),
    )
    tables = routed([live["t" + name] for name in near], half // LANES)
    live = phase(live, {}, far=("tr1", "tq2", "tq3"), near=tables)
    live = phase(
        live,
        dict(tr2=("tq2", "x"), tr3=("tr1", "y"), cq1=("cq0", "ahead"), down=("down", "core")),
        near_values=enter_tokens(live, near),
    )
    tables = routed([live["t" + name] for name in late], half // LANES)
    live["hidden"] = live["near_values"][0]
    live = phase(live, {}, far=("tr2", "tr3", "hidden"), late=tables)
    live = phase(
        live,
        dict(cq2=("cq1", "ahead"), cr1=("cq1", "x"), cq3=("cq1", "y"), gate=("gate", "core")),
        far=("cq1",),
        late_values=enter_tokens(live, late),
    )
    live = {name: value for name, value in live.items() if name[0] != "t"}
    live["late_hidden"] = live["late_values"][0]
    live = phase(live, {}, far=("late_hidden", "cq2", "cr1", "cq3"))
    tables = [live["near"][3], live["late"][3]]
    names = ("hidden", "hidden_far", "late_hidden", "late_hidden_far")
    live = phase(
        live,
        dict(cr0=("cq0", "x"), cr2=("cr1", "ahead"), cr3=("cr1", "y"), up=("up", "core")),
        o=leave(live["mine"], tables, [live[name] for name in names], (w_down, live["down"])),
    )
    live.update({"o" + name: block(live, "o", name) for name in ("r3", "r2", "r0")})
    live = phase(live, {}, far=("cr0", "cr2", "cr3"))
    tables = [live["near"][1], live["late"][1]]
    factors = list(live["near_values"][1:]) + list(live["late_values"][1:])
    left, right = enter(True, live["mine"], tables, pieces(live, "c", order), (w_down,), factors)
    place_t = [live["near"][2], live["late"][2]]
    live = {name: value for name, value in live.items() if name[0] in "mogu"}
    live = phase(
        live,
        dict(oy=("or3", "y"), oz=("or2", "back"), ox=("or0", "x")),
        left=left,
        right=right,
    )
    live = phase(
        live,
        {},
        far=("left", "right"),
        or1=add(block(live, "o", "r1"), live["oy"], live["oz"]),
        oq3=block(live, "o", "q3"),
        oq2=block(live, "o", "q2"),
    )
    weights = (w_gate, w_up, live["gate"], live["up"])
    names = ("left", "right", "left_far", "right_far")
    live = phase(
        live,
        dict(oy=("oq3", "y"), oq=("or1", "x"), oz=("oq2", "back")),
        g=leave(live["mine"], place_t, [live[name] for name in names], weights),
    )
    slack = move(add(block(live, "o", "q1"), live["oy"], live["oq"], live["oz"]), "back")
    live.update({"g" + name: block(live, "g", name) for name in ("r3", "r2")})
    live = phase(
        live,
        dict(gy=("gr3", "y"), gx=("gr2", "x")),
        gq3=block(live, "g", "q3"),
        gr0=block(live, "g", "r0"),
    )
    live["oz"] = slack
    live["gr1"] = add(block(live, "g", "r1"), live["gy"])
    live["gq2"] = add(block(live, "g", "q2"), live["gx"])
    live = phase(
        live,
        dict(gy=("gq3", "y"), gx=("gr1", "x"), gz=("gq2", "back")),
        mixed=add(block(live, "o", "q0"), live["ox"], live["oz"]),
    )
    slack = move(live["mixed"], "y")
    live["gq1"] = add(block(live, "g", "q1"), live["gy"], live["gx"], live["gz"])
    live = phase(live, dict(gz=("gq1", "back"), gx=("gr0", "x")))
    live["oy"] = slack
    live["grad"] = add(block(live, "g", "q0"), live["gx"], live["gz"])
    live = phase(
        live, dict(gy=("grad", "y")), mixed=whole_rows(add(live["mixed"], live["oy"]), core)
    )
    return live["mixed"], whole_rows(add(live["grad"], live["gy"]), core)


def whole_rows(own, core):
    far = move(own, "core")
    return jnp.concatenate([jnp.where(core == 0, own, far), jnp.where(core == 0, far, own)], axis=1)


def solution(mesh):
    fast = mesh.shape["expert"] == 8 and mesh.shape["tensor"] == 4
    return jax.shard_map(
        functools.partial(body, fast),
        mesh=mesh,
        in_specs=(
            P("expert", None),
            P("expert", None),
            P("expert", None),
            P("expert", None),
            P("expert", "tensor", None),
            P("expert", "tensor", None),
            P("expert", "tensor", None),
        ),
        out_specs=(P("expert", None), P("expert", None)),
        check_vma=False,
    )
```

```python
import functools

import jax
import jax.numpy as jnp
import numpy as np
from jax import lax
from jax.experimental import pallas as pl
from jax.experimental.pallas import tpu as pltpu
from jax.sharding import PartitionSpec as P

AXES = ("expert", "tensor")
CHUNK = 512
ROW_TILE = 16
LANES = 128


def chip_moves():
    def pairs(step):
        found = []
        for z in range(4):
            for x in range(2):
                for y in range(2):
                    for core in range(2):
                        to_z, to_x, to_y, to_core = step(z, x, y, core)
                        source = (z * 2 + x) * 4 + y * 2 + core
                        found.append((source, ((to_z % 4) * 2 + to_x) * 4 + to_y * 2 + to_core))
        return found

    return dict(
        ahead=pairs(lambda z, x, y, core: (z + 1 - 2 * y, x, y, core)),
        back=pairs(lambda z, x, y, core: (z - 1 + 2 * y, x, y, core)),
        x=pairs(lambda z, x, y, core: (z, 1 - x, y, core)),
        y=pairs(lambda z, x, y, core: (z, x, 1 - y, core)),
        core=pairs(lambda z, x, y, core: (z, x, y, 1 - core)),
    )


MOVES = chip_moves()


def move(array, name):
    return lax.ppermute(array, AXES, MOVES[name])


def add(*terms):
    total = terms[0].astype(jnp.float32)
    for term in terms[1:]:
        total = total + term.astype(jnp.float32)
    return total.astype(jnp.bfloat16)


def halves(array, core):
    half = array.shape[1] // 2
    return [
        lax.dynamic_slice_in_dim(array, side * half, half, 1) for side in (core, 1 - core)
    ]


def table_copies(refs, table_ref, sem_ref):
    copies, start = [], 0
    for n, ref in enumerate(refs):
        place = table_ref.at[pl.ds(start, ref.shape[0])]
        copies.append(pltpu.make_async_copy(ref, place, sem_ref.at[n]))
        start += ref.shape[0]
    return copies


def enter_kernel(backward, parts, sources, group, slots, half, *refs):
    count = 1 if backward else 2
    core_ref = refs[0]
    place_refs = refs[1 : 1 + parts]
    piece_refs = refs[1 + parts : 1 + parts + 2 * sources]
    weight_refs = refs[1 + parts + 2 * sources : 1 + parts + 2 * sources + count]
    if backward:
        factor_refs, (left_ref, right_ref) = refs[1 + parts + 2 * sources + count : -9], refs[-9:-7]
    else:
        left_ref, first_ref, second_ref = refs[-10:-7]
    block_ref, rows_ref, buffer_ref, table_ref, sem_ref, weight_sem_ref, table_sem_ref = refs[-7:]
    step = pl.program_id(0)
    core = core_ref[0]
    experts = rows_ref.shape[0]
    depth = buffer_ref.shape[1]
    tokens = block_ref.shape[1] // sources
    span = group * tokens
    nt = (((1,), (1,)), ((), ()))

    def piece_copy(side, j):
        return pltpu.make_async_copy(
            piece_refs[side * sources + j].at[:, pl.ds(0, half)],
            block_ref.at[side, pl.ds(j * tokens, tokens)],
            sem_ref.at[side * sources + j],
        )

    def weight_copy(n, expert):
        slot = lax.rem(expert, depth)
        return pltpu.make_async_copy(
            weight_refs[n].at[expert], buffer_ref.at[n, slot], weight_sem_ref.at[n, slot]
        )

    @pl.when(step == 0)
    def _():
        tables = table_copies(place_refs, table_ref, table_sem_ref)
        for copy in tables:
            copy.start()
        for k in range(sources // group):
            for side in range(2):
                for j in range(k * group, (k + 1) * group):
                    piece_copy(side, j).start()
        for copy in tables:
            copy.wait()
        for k in range(sources // group):
            for side in range(2):
                for j in range(k * group, (k + 1) * group):
                    piece_copy(side, j).wait()
                if 2 * k + side < depth:
                    for n in range(count):
                        weight_copy(n, 2 * k + side).start()
                base = (core if side == 0 else 1 - core) * half
                for column in range(0, half, CHUNK):
                    block = block_ref[side, pl.ds(k * span, span), pl.ds(column, CHUNK)]
                    picked = jnp.dot(table_ref[k], block, preferred_element_type=jnp.float32)
                    to = pl.multiple_of(base + column, CHUNK)
                    rows_ref[:, pl.ds(k * slots, slots), pl.ds(to, CHUNK)] = picked.astype(
                        jnp.bfloat16
                    ).reshape(experts, slots, CHUNK)

    for n in range(count):
        weight_copy(n, step).wait()
    rows = rows_ref[step]
    slot = lax.rem(step, depth)
    products = [
        lax.dot_general(rows, buffer_ref[n, slot], nt, preferred_element_type=jnp.float32)
        for n in range(count)
    ]
    if backward:
        start = 0
        for first_ref, second_ref in zip(factor_refs[0::2], factor_refs[1::2]):
            span_rows = pl.ds(start, first_ref.shape[1])
            product = products[0][start : start + first_ref.shape[1]]
            left_ref[0, span_rows] = (product * first_ref[0]).astype(jnp.bfloat16)
            right_ref[0, span_rows] = (product * second_ref[0]).astype(jnp.bfloat16)
            start += first_ref.shape[1]
    else:
        pre_gate, up_value = products
        sigmoid = jax.nn.sigmoid(pre_gate)
        activated = pre_gate * sigmoid
        left_ref[0] = (activated * up_value).astype(jnp.bfloat16)
        first_ref[0] = up_value * sigmoid * (1.0 + pre_gate * (1.0 - sigmoid))
        second_ref[0] = activated

    @pl.when(step + depth < experts)
    def _():
        for n in range(count):
            weight_copy(n, step + depth).start()


def enter(backward, core, places, pieces, weights, factors):
    experts, hidden, features = weights[0].shape
    sources = len(pieces) // 2
    tokens, half = pieces[0].shape[0], features // 2
    _, height, span = places[0].shape
    groups = sum(place.shape[0] for place in places)
    slots = height // experts
    total = groups * slots
    depth = min(3, experts, 2 * groups)
    per_expert = pl.BlockSpec((1, total, hidden), lambda i, c: (i, 0, 0))
    in_specs = [pl.BlockSpec(memory_space=pl.ANY)] * (len(places) + 2 * sources + len(weights))
    in_specs += [
        pl.BlockSpec((1,) + factor.shape[1:], lambda i, c: (i, 0, 0)) for factor in factors
    ]
    values = jax.ShapeDtypeStruct((experts, total, hidden), jnp.bfloat16)
    exact = jax.ShapeDtypeStruct((experts, total, hidden), jnp.float32)
    out_shape = [values, values] if backward else [values, exact, exact]
    return pl.pallas_call(
        functools.partial(enter_kernel, backward, len(places), sources, span // tokens, slots, half),
        grid_spec=pltpu.PrefetchScalarGridSpec(
            num_scalar_prefetch=1,
            grid=(experts,),
            in_specs=in_specs,
            out_specs=[per_expert] * len(out_shape),
            scratch_shapes=[
                pltpu.VMEM((2, sources * tokens, half), jnp.bfloat16),
                pltpu.VMEM((experts, total, features), jnp.bfloat16),
                pltpu.VMEM((len(weights), depth, hidden, features), jnp.bfloat16),
                pltpu.VMEM((groups, height, span), jnp.bfloat16),
                pltpu.SemaphoreType.DMA((2 * sources,)),
                pltpu.SemaphoreType.DMA((len(weights), depth)),
                pltpu.SemaphoreType.DMA((len(places),)),
            ],
        ),
        out_shape=out_shape,
        compiler_params=pltpu.CompilerParams(vmem_limit_bytes=(38 if backward else 46) * 1024 * 1024),
        cost_estimate=pl.CostEstimate(
            flops=128 * features * (len(weights) * experts * total * hidden + groups * height * span),
            bytes_accessed=len(weights) * experts * hidden * features * 2
            + 2 * sources * tokens * features,
            transcendentals=0,
        ),
        name="enter_backward" if backward else "enter_forward",
    )(core, *places, *pieces, *weights, *factors)


def leave_kernel(parts, count, *refs):
    place_refs = refs[1 : 1 + parts]
    value_refs = refs[1 + parts : -2 - count]
    weight_refs = refs[-2 - count : -2]
    out_ref, rows_ref = refs[-2:]
    step = pl.program_id(0)
    experts, total, half = rows_ref.shape
    _, span, height = place_refs[0].shape
    places = [ref.at[k] for ref in place_refs for k in range(ref.shape[0])]
    slots = height // experts
    width = out_ref.shape[1]
    each = refs[-3].shape[0]
    turns = experts // each

    @pl.when(step < turns)
    def _():
        for n in range(each):
            expert = step * each + n
            values = [
                jnp.concatenate([ref[expert] for ref in value_refs[m::count]], axis=0)
                for m in range(count)
            ]
            for column in range(0, half, CHUNK):
                columns = pl.ds(column, CHUNK)
                result = sum(
                    jnp.dot(value, ref[n, :, columns], preferred_element_type=jnp.float32)
                    for value, ref in zip(values, weight_refs)
                )
                rows_ref[expert, :, columns] = result.astype(jnp.bfloat16)

    @pl.when(step >= turns)
    def _():
        base = (step - turns) * width
        for column in range(0, width, CHUNK // 2):
            columns = pl.ds(pl.multiple_of(base + column, CHUNK // 2), CHUNK // 2)
            for k in range(len(places)):
                rows = rows_ref[:, pl.ds(k * slots, slots), columns].reshape(height, CHUNK // 2)
                out_ref[pl.ds(k * span, span), pl.ds(column, CHUNK // 2)] = jnp.dot(
                    places[k][...], rows, preferred_element_type=jnp.float32
                ).astype(jnp.bfloat16)


def leave(side, places, values, weights):
    experts, hidden, features = weights[0].shape
    _, span, height = places[0].shape
    groups = sum(place.shape[0] for place in places)
    total = groups * (height // experts)
    half = features // 2
    width = half // 2
    each = 2 if experts % 2 == 0 else 1
    turns = experts // each
    whole = lambda shape: pl.BlockSpec(shape, lambda i, s: (0,) * len(shape))
    return pl.pallas_call(
        functools.partial(leave_kernel, len(places), len(weights)),
        grid_spec=pltpu.PrefetchScalarGridSpec(
            num_scalar_prefetch=1,
            grid=(turns + half // width,),
            in_specs=[whole(array.shape) for array in list(places) + list(values)]
            + [
                pl.BlockSpec(
                    (each, hidden, half),
                    functools.partial(
                        lambda wide, i, s: (jnp.minimum(i, turns - 1), 0, s[0] * wide),
                        int(weight.shape[2] > half),
                    ),
                )
                for weight in weights
            ],
            out_specs=pl.BlockSpec(
                (groups * span, width), lambda i, s: (0, jnp.maximum(i - turns, 0))
            ),
            scratch_shapes=[pltpu.VMEM((experts, total, half), jnp.bfloat16)],
        ),
        out_shape=jax.ShapeDtypeStruct((groups * span, half), jnp.bfloat16),
        compiler_params=pltpu.CompilerParams(vmem_limit_bytes=(46 if len(weights) < 4 else 40) * 1024 * 1024),
        cost_estimate=pl.CostEstimate(
            flops=128 * half * (len(weights) * experts * total * hidden + groups * height * span),
            bytes_accessed=len(weights) * experts * hidden * half * 2 + 2 * groups * span * half,
            transcendentals=0,
        ),
        name="leave",
    )(side, *places, *values, *weights)


def choice_columns(expert_ids, gate_probs):
    columns = jnp.concatenate([expert_ids.astype(jnp.float32), gate_probs], axis=1)
    columns = jnp.pad(columns, ((0, 0), (0, LANES - columns.shape[1])))
    return columns.astype(jnp.bfloat16)


def first_kernel(core_ref, half_ref, ids_ref, probs_ref, out_ref):
    tokens, half = half_ref.shape
    out_ref[:, pl.ds(0, half)] = half_ref[...]
    ids, probs = ids_ref[...].astype(jnp.float32), probs_ref[...]
    rest = jnp.zeros((LANES - 2 * ids.shape[0], tokens), jnp.float32)
    columns = jnp.concatenate([ids, probs, rest], axis=0).T
    out_ref[:, pl.ds(half, LANES)] = columns.astype(jnp.bfloat16)


def first_piece(core, tokens, expert_ids, gate_probs):
    count, features = tokens.shape
    half = features // 2
    whole = pl.BlockSpec((expert_ids.shape[1], count), lambda i, c: (0, 0))
    return pl.pallas_call(
        first_kernel,
        grid_spec=pltpu.PrefetchScalarGridSpec(
            num_scalar_prefetch=1,
            grid=(1,),
            in_specs=[pl.BlockSpec((count, half), lambda i, c: (0, c[0])), whole, whole],
            out_specs=pl.BlockSpec((count, half + LANES), lambda i, c: (0, 0)),
        ),
        out_shape=jax.ShapeDtypeStruct((count, half + LANES), jnp.bfloat16),
        name="first_piece",
    )(core, tokens, expert_ids.T, gate_probs.T)


def route_kernel(sources, group, capacity, *refs):
    first_ref = refs[0]
    choice_refs = refs[1 : 1 + sources]
    ids_ref, probs_ref, rows_ref, earlier_ref, expert_ref, slot_ref = refs[1 + sources : 7 + sources]
    place_ref, place_prob_ref, place_t_ref, place_t_prob_ref = refs[7 + sources :]
    tokens = earlier_ref.shape[0]
    dot = functools.partial(jnp.dot, preferred_element_type=jnp.float32)
    sought = expert_ref[...] + first_ref[0].astype(jnp.float32)
    for j in range(sources):
        k, s = divmod(j, group)
        choice = choice_refs[j][...]
        match = dot(choice, ids_ref[...]) == sought
        weight = jnp.where(match, dot(choice, probs_ref[...]), 0.0).astype(jnp.bfloat16)
        chosen = dot(jnp.where(match, 1.0, 0.0).astype(jnp.bfloat16), rows_ref[...])
        weight = dot(weight, rows_ref[...])
        position = dot(earlier_ref[...], chosen.astype(jnp.bfloat16)) + float(s * capacity)
        here = (chosen > 0.5) & (position == slot_ref[...])
        plain = jnp.where(here, 1.0, 0.0)
        weighted = jnp.where(here, weight, 0.0)
        span = pl.ds(s * tokens, tokens)
        place_t_ref[k, span, :] = plain.astype(jnp.bfloat16)
        place_t_prob_ref[k, span, :] = weighted.astype(jnp.bfloat16)
        place_ref[k, :, span] = plain.T.astype(jnp.bfloat16)
        place_prob_ref[k, :, span] = weighted.T.astype(jnp.bfloat16)


def route(first, choices, column, top, experts, capacity, group):
    sources, tokens = len(choices), choices[0].shape[0]
    groups = sources // group
    slots = -(-group * capacity // ROW_TILE) * ROW_TILE
    height, span = experts * slots, group * tokens
    lanes = np.arange(top * experts)
    rows = np.arange(height)
    columns = np.arange(LANES)[:, None]
    tables = [
        (columns == lanes // experts),
        (columns == lanes // experts + top),
        (lanes[:, None] % experts == rows // slots),
        (np.arange(tokens)[:, None] > np.arange(tokens)),
    ]
    tables = [jnp.asarray(table.astype(np.float32), jnp.bfloat16) for table in tables]
    tables += [
        jnp.asarray((lanes % experts).astype(np.float32)[None]),
        jnp.asarray((rows % slots).astype(np.float32)[None]),
    ]
    whole = lambda shape: pl.BlockSpec(shape, lambda i, f: (0,) * len(shape))
    by_row = jax.ShapeDtypeStruct((groups, height, span), jnp.bfloat16)
    by_token = jax.ShapeDtypeStruct((groups, span, height), jnp.bfloat16)
    out_shape = [by_row, by_row, by_token, by_token]
    return pl.pallas_call(
        functools.partial(route_kernel, sources, group, capacity),
        grid_spec=pltpu.PrefetchScalarGridSpec(
            num_scalar_prefetch=1,
            grid=(1,),
            in_specs=[pl.BlockSpec((tokens, LANES), lambda i, f: (0, column))] * sources
            + [whole(table.shape) for table in tables],
            out_specs=[whole(shape.shape) for shape in out_shape],
        ),
        out_shape=out_shape,
        compiler_params=pltpu.CompilerParams(vmem_limit_bytes=32 * 1024 * 1024),
        name="route",
    )(first, *choices, *tables)


def body(fast, tokens, cotangent, expert_ids, gate_probs, w_gate, w_up, w_down):
    tok_count, features = tokens.shape
    top = expert_ids.shape[1]
    expert_devs = lax.axis_size("expert")
    local_experts = w_gate.shape[0]
    capacity = max(2, 9 * tok_count * top // (8 * local_experts * expert_devs))
    group = max(1, expert_devs // 4)
    half = features // 2
    first = (lax.axis_index("expert") * local_experts).astype(jnp.int32).reshape(1)
    routed = functools.partial(
        route, first, top=top, experts=local_experts, capacity=capacity, group=group
    )
    own_choices = choice_columns(expert_ids, gate_probs)
    if fast:
        return exchange(
            routed, expert_ids, gate_probs, tokens, cotangent, w_gate, w_up, w_down
        )

    def split(array):
        blocks = lax.all_gather(array, "expert")
        return [
            blocks[j, :, side * half : (side + 1) * half]
            for side in range(2)
            for j in range(expert_devs)
        ]

    choices = lax.all_gather(own_choices, "expert")
    place, place_prob, place_t, place_t_prob = routed([choices[j] for j in range(expert_devs)], 0)
    zero = jnp.zeros((1,), jnp.int32)
    hidden, *factors = enter(False, zero, [place], split(tokens), (w_gate, w_up), ())
    values = enter(True, zero, [place_prob], split(cotangent), (w_down,), factors)

    def total(table, values, weights):
        partial = jnp.concatenate(
            [leave(zero + side, [table], values, weights) for side in range(2)], axis=1
        )
        own = lax.psum_scatter(partial, "expert", scatter_dimension=0, tiled=True)
        return lax.psum(own, "tensor")

    return total(place_t_prob, (hidden,), (w_down,)), total(place_t, values, (w_gate, w_up))


def exchange(routed, expert_ids, gate_probs, tokens, cotangent, w_gate, w_up, w_down):
    half = tokens.shape[1] // 2
    core = lax.axis_index("tensor") % 2
    mine = core.astype(jnp.int32).reshape(1)
    order = ("q0", "r0", "q1", "r1", "q2", "r2", "q3", "r3")

    def phase(live, moves, far=(), **made):
        moved = {name: move(live[old], how) for name, (old, how) in moves.items()}
        moved.update({name + "_far": move(live[name], "core") for name in far})
        return lax.optimization_barrier({**live, **moved, **made})

    def pieces(live, kind, names):
        return [live[kind + name] for name in names] + [live[kind + name + "_far"] for name in names]

    def enter_tokens(live, names):
        tables = live["near" if names is near else "late"]
        return enter(False, live["mine"], tables[:1], pieces(live, "t", names), (w_gate, w_up), ())

    def sibling_half(weight):
        return lax.dynamic_slice_in_dim(weight, (1 - core) * half, half, 2)

    def block(live, kind, name):
        rows = tokens.shape[0]
        start = order.index(name) * rows
        return live[kind][start : start + rows]

    near, late = order[:4], order[4:]
    tq0 = first_piece(mine, tokens, expert_ids, gate_probs)
    live = dict(mine=mine, tq0=tq0, tq0_far=halves(tokens, core)[1])
    cq0, cq0_far = halves(cotangent, core)
    live = phase(
        live,
        dict(tq1=("tq0", "ahead"), tr0=("tq0", "x")),
        cq0=cq0,
        cq0_far=cq0_far,
        down=sibling_half(w_down),
        gate=sibling_half(w_gate),
    )
    live = phase(
        live,
        dict(tq2=("tq1", "ahead"), tr1=("tq1", "x"), tq3=("tq1", "y")),
        far=("tr0", "tq1"),
        up=sibling_half(w_up),
    )
    tables = routed([live["t" + name] for name in near], half // LANES)
    live = phase(live, {}, far=("tr1", "tq2", "tq3"), near=tables)
    live = phase(
        live,
        dict(tr2=("tq2", "x"), tr3=("tr1", "y"), cq1=("cq0", "ahead"), down=("down", "core")),
        near_values=enter_tokens(live, near),
    )
    tables = routed([live["t" + name] for name in late], half // LANES)
    live["hidden"] = live["near_values"][0]
    live = phase(live, {}, far=("tr2", "tr3", "hidden"), late=tables)
    live = phase(
        live,
        dict(cq2=("cq1", "ahead"), cr1=("cq1", "x"), cq3=("cq1", "y"), gate=("gate", "core")),
        far=("cq1",),
        late_values=enter_tokens(live, late),
    )
    live = {name: value for name, value in live.items() if name[0] != "t"}
    live["late_hidden"] = live["late_values"][0]
    live = phase(live, {}, far=("late_hidden", "cq2", "cr1", "cq3"))
    tables = [live["near"][3], live["late"][3]]
    names = ("hidden", "hidden_far", "late_hidden", "late_hidden_far")
    live = phase(
        live,
        dict(cr0=("cq0", "x"), cr2=("cr1", "ahead"), cr3=("cr1", "y"), up=("up", "core")),
        o=leave(live["mine"], tables, [live[name] for name in names], (w_down, live["down"])),
    )
    live.update({"o" + name: block(live, "o", name) for name in ("r3", "r2", "r0")})
    live = phase(live, {}, far=("cr0", "cr2", "cr3"))
    tables = [live["near"][1], live["late"][1]]
    factors = list(live["near_values"][1:]) + list(live["late_values"][1:])
    left, right = enter(True, live["mine"], tables, pieces(live, "c", order), (w_down,), factors)
    place_t = [live["near"][2], live["late"][2]]
    live = {name: value for name, value in live.items() if name[0] in "mogu"}
    live = phase(
        live,
        dict(oy=("or3", "y"), oz=("or2", "back"), ox=("or0", "x")),
        left=left,
        right=right,
    )
    live = phase(
        live,
        {},
        far=("left", "right"),
        or1=add(block(live, "o", "r1"), live["oy"], live["oz"]),
        oq3=block(live, "o", "q3"),
        oq2=block(live, "o", "q2"),
    )
    weights = (w_gate, w_up, live["gate"], live["up"])
    names = ("left", "right", "left_far", "right_far")
    live = phase(
        live,
        dict(oy=("oq3", "y"), oq=("or1", "x"), oz=("oq2", "back")),
        g=leave(live["mine"], place_t, [live[name] for name in names], weights),
    )
    slack = move(add(block(live, "o", "q1"), live["oy"], live["oq"], live["oz"]), "back")
    live.update({"g" + name: block(live, "g", name) for name in ("r3", "r2")})
    live = phase(
        live,
        dict(gy=("gr3", "y"), gx=("gr2", "x")),
        gq3=block(live, "g", "q3"),
        gr0=block(live, "g", "r0"),
    )
    live["oz"] = slack
    live["gr1"] = add(block(live, "g", "r1"), live["gy"])
    live["gq2"] = add(block(live, "g", "q2"), live["gx"])
    live = phase(
        live,
        dict(gy=("gq3", "y"), gx=("gr1", "x"), gz=("gq2", "back")),
        mixed=add(block(live, "o", "q0"), live["ox"], live["oz"]),
    )
    slack = move(live["mixed"], "y")
    live["gq1"] = add(block(live, "g", "q1"), live["gy"], live["gx"], live["gz"])
    live = phase(live, dict(gz=("gq1", "back"), gx=("gr0", "x")))
    live["oy"] = slack
    live["grad"] = add(block(live, "g", "q0"), live["gx"], live["gz"])
    live = phase(
        live, dict(gy=("grad", "y")), mixed=whole_rows(add(live["mixed"], live["oy"]), core)
    )
    return live["mixed"], whole_rows(add(live["grad"], live["gy"]), core)


def whole_rows(own, core):
    far = move(own, "core")
    return jnp.concatenate([jnp.where(core == 0, own, far), jnp.where(core == 0, far, own)], axis=1)


def solution(mesh):
    fast = mesh.shape["expert"] == 8 and mesh.shape["tensor"] == 4
    return jax.shard_map(
        functools.partial(body, fast),
        mesh=mesh,
        in_specs=(
            P("expert", None),
            P("expert", None),
            P("expert", None),
            P("expert", None),
            P("expert", "tensor", None),
            P("expert", "tensor", None),
            P("expert", "tensor", None),
        ),
        out_specs=(P("expert", None), P("expert", None)),
        check_vma=False,
    )
```
